128 devices in a mesh: blk: 16 (over x, z), group: 8 (over y, core).
Axes of the slice: x: 4, y: 4, z: 4, core: 2. Of those that a mesh axis runs over, the one named last changes fastest.
Arguments:
- activations: bfloat16 [524288, 2048], P(('blk', 'group')), may hold values from -8 to 8
- grad_out: bfloat16 [524288, 512], P(('blk', 'group')), may hold values from -8 to 8
- weights: float32 [2048, 512], P(('blk', 'group')), may hold values from -6 to 6
- momentum: float32 [2048, 512], P(('blk', 'group')), may hold values from -6 to 6
Outputs:
- new_weights: float32 [2048, 512], P(('blk', 'group'))
- new_momentum: float32 [2048, 512], P(('blk', 'group'))
The draws below stay inside these ranges and needn't reach their ends.
All inputs are finite; a program needn't handle non-finite values.
Results may differ from the reference program's by a relative error of at most 0.0003.
Values sent between devices are 32-bit elements; how exact they have to be, the bound alone decides.
No kernel may reach another device: no remote copies, remote signals or barrier semaphores. Data moves between devices by JAX's collectives and lax.ppermute only.
A program may use at most 128 MiB of HBM per device.

```python
import math
import jax
import jax.numpy as jnp
from jax import lax

D = 2048
COLS = 512
TOK_DEV = 4096
TOKENS = 524288
LEVELS = 3
N_BLK = 16
N_GROUP = 8


def draw_common(key, width, salt):
    noise_key, offset_key = jax.random.split(jax.random.fold_in(key, salt), 2)
    noise = jax.random.normal(noise_key, (TOKENS, width), jnp.float32)
    offset = jax.random.normal(offset_key, (width,), jnp.float32) * (TOK_DEV * 16.0) ** (-0.25)
    drawn = noise + offset
    return jnp.clip(drawn, -8.0, 8.0)


def draw_activations(key, part):
    return draw_common(key, D, 11).astype(jnp.bfloat16)


def draw_grad_out(key, part):
    return draw_common(key, COLS, 23).astype(jnp.bfloat16)


def steps_of(stream_key, shape, cuts, low, top_value):
    gain, own = 1.0, jax.random.fold_in(stream_key, 6)
    for axis_at, blocks in cuts:
        draws = jnp.exp(jax.random.uniform(jax.random.fold_in(own, axis_at), (blocks,), jnp.float32, low / len(cuts), top_value / len(cuts)))
        gain = gain * jnp.repeat(draws, shape[axis_at] // blocks).reshape([-1 if axis == axis_at else 1 for axis in range(len(shape))])
    return gain


def centred(own_key, shape, scale, limit, pieces=(), kind=jnp.bfloat16):
    loudness = steps_of(own_key, shape, pieces, -0.22, 0.18) if pieces else 1.0
    values = jax.random.normal(own_key, shape, jnp.float32) * scale * loudness
    return jnp.minimum(jnp.maximum(values, -limit), limit).astype(kind)


def setup_inputs(seed: int = 0) -> dict:
    splits = jax.random.split(jax.random.key(seed), 5)
    activations = draw_activations(jax.random.fold_in(splits[4], 71), 0)
    grad_out = draw_grad_out(jax.random.fold_in(splits[4], 71), 0)
    weights = centred(splits[2], (D, COLS), 1.0, 6.0, ((0, 128),), jnp.float32)
    momentum = centred(splits[3], (D, COLS), 1.0, 6.0, ((0, 128),), jnp.float32)
    return dict(activations=activations, grad_out=grad_out, weights=weights, momentum=momentum)


epsilon = 1e-06

def reference(activations, grad_out, weights, momentum):
    act_blocks = activations.reshape(N_BLK, N_GROUP, TOK_DEV, D)
    out_blocks = grad_out.reshape(N_BLK, N_GROUP, TOK_DEV, COLS)
    grad_scale = 1.0 / math.sqrt(TOK_DEV * N_BLK)

    def group_grad(group_index):
        act_group = lax.dynamic_index_in_dim(act_blocks, group_index, 1, keepdims=False).reshape(N_BLK * TOK_DEV, D)
        out_group = lax.dynamic_index_in_dim(out_blocks, group_index, 1, keepdims=False).reshape(N_BLK * TOK_DEV, COLS)
        return jnp.dot(act_group.T, out_group, preferred_element_type=jnp.float32) * grad_scale
    stacked = lax.map(group_grad, jnp.arange(N_GROUP, dtype=jnp.int32))
    for level_step in range(LEVELS):
        half_rows = stacked.shape[0] // 2
        lower_half = stacked[:half_rows]
        upper_half = stacked[half_rows:]
        inner_prod = lax.optimization_barrier(jnp.sum(lower_half * upper_half, axis=(1, 2)))
        lower_sq = lax.optimization_barrier(jnp.sum(lower_half * lower_half, axis=(1, 2)))
        upper_sq = lax.optimization_barrier(jnp.sum(upper_half * upper_half, axis=(1, 2)))
        coef_lower = 1.0 - inner_prod / (2.0 * (lower_sq + epsilon))
        coef_upper = 1.0 - inner_prod / (2.0 * (upper_sq + epsilon))
        stacked = coef_lower[:, None, None] * lower_half + coef_upper[:, None, None] * upper_half
    combined = stacked[0]
    new_momentum = 0.9 * momentum + combined
    new_weights = (1.0 - 0.1 * 0.1) * weights - 0.1 * new_momentum
    return (new_weights, new_momentum)
```

```python
import math

import jax
import jax.numpy as jnp
from jax import lax
from jax.experimental import pallas as pl
from jax.experimental.pallas import tpu as pltpu
from jax.sharding import PartitionSpec as P

EPSILON = 1e-06
GROUPS = 8
SIDE = 4
ROWS = 16
HALF = 256
PIECE = GROUPS * ROWS
TOTAL = 128
CONTRACT = (((0,), (0,)), ((), ()))


def exchanged(value, axis, mask):
    return lax.ppermute(value, axis, [(k, k ^ mask) for k in range(lax.axis_size(axis))])


def pair_slots():
    return [(i, j) for i in range(GROUPS) for j in range(i, GROUPS)]


def gram_kernel(place_ref, *refs):
    *block_refs, sums_ref, ordered_ref = refs
    y = place_ref[0]
    slots = [[block_ref[core] for core in range(2)] for block_ref in block_refs]
    for bit in (1, 2):
        moved = (y & bit) != 0
        slots = [
            [jnp.where(moved, slots[k ^ bit][core], slots[k][core]) for core in range(2)]
            for k in range(SIDE)
        ]
    groups = [slots[i // 2][i % 2] for i in range(GROUPS)]
    for i in range(GROUPS):
        ordered_ref[i] = groups[i]
    rows = []
    for i, j in pair_slots():
        product = groups[i] * groups[j]
        product = product[0] + product[1]
        product = product[:8] + product[8:]
        product = product[:, :128] + product[:, 128:]
        rows.append(jnp.sum(product, axis=0, keepdims=True))
    rows.append(jnp.zeros((128 - len(rows), 128), jnp.float32))
    sums_ref[...] = lax.dot_general(
        jnp.ones((TOTAL, 128), jnp.float32),
        jnp.concatenate(rows, axis=0),
        (((1,), (1,)), ((), ())),
        precision=lax.Precision.HIGHEST,
        preferred_element_type=jnp.float32,
    )


def finish_kernel(sums_ref, ordered_ref, weights_ref, momentum_ref, new_weights_ref, new_momentum_ref):
    sums = jnp.sum(sums_ref[...], axis=0, keepdims=True)
    gram = {}
    for place, (i, j) in enumerate(pair_slots()):
        gram[i, j] = gram[j, i] = sums[:, place : place + 1]
    shares = [1.0] * GROUPS
    count = GROUPS
    while count > 1:
        half = count // 2
        coef = [None] * count
        for i in range(half):
            cross = gram[i, i + half]
            coef[i] = 1.0 - cross / (2.0 * (jnp.maximum(gram[i, i], 0.0) + EPSILON))
            coef[i + half] = 1.0 - cross / (2.0 * (jnp.maximum(gram[i + half, i + half], 0.0) + EPSILON))
        shares = [shares[g] * coef[g % count] for g in range(GROUPS)]
        later = {}
        for i in range(half):
            for j in range(i, half):
                later[i, j] = later[j, i] = (
                    coef[i] * coef[j] * gram[i, j]
                    + coef[i + half] * coef[j + half] * gram[i + half, j + half]
                ) + (
                    coef[i] * coef[j + half] * gram[i, j + half]
                    + coef[i + half] * coef[j] * gram[i + half, j]
                )
        gram = later
        count = half
    for part in range(2):
        columns = slice(part * HALF, (part + 1) * HALF)
        combined = shares[0] * ordered_ref[0, part]
        for i in range(1, GROUPS):
            combined = combined + shares[i] * ordered_ref[i, part]
        new_momentum = 0.9 * momentum_ref[:, columns] + combined
        new_momentum_ref[:, columns] = new_momentum
        new_weights_ref[:, columns] = (1.0 - 0.1 * 0.1) * weights_ref[:, columns] - 0.1 * new_momentum


def in_vmem(count):
    return [pl.BlockSpec(memory_space=pltpu.VMEM)] * count


def shards(activations, grad_out, weights, momentum):
    blk = lax.axis_index("blk")
    group = lax.axis_index("group")
    x, z = blk // SIDE, blk % SIDE
    y, core = group // 2, group % 2
    grad_scale = 1.0 / math.sqrt(activations.shape[0] * lax.axis_size("blk"))
    grad = lax.dot_general(activations, grad_out, CONTRACT, preferred_element_type=jnp.float32)
    part_a = grad[:, :HALF].reshape(SIDE, SIDE, PIECE, HALF)
    part_b = grad[:, HALF:].reshape(SIDE, SIDE, PIECE, HALF)

    def taken(value, index, dim):
        return lax.dynamic_index_in_dim(value, index, dim, keepdims=False)

    def reduced(value_a, place_a, dim_a, mask_a, value_b, place_b, dim_b, mask_b):
        arrived_a, arrived_b = [], []
        for s in (2, 1, 3):
            arrived_a.append(exchanged(taken(value_a, place_a ^ s, dim_a), "blk", s * mask_a))
            arrived_b.append(exchanged(taken(value_b, place_b ^ s, dim_b), "blk", s * mask_b))
        sum_a = taken(value_a, place_a, dim_a) + arrived_a[0] + arrived_a[1] + arrived_a[2]
        sum_b = taken(value_b, place_b, dim_b) + arrived_b[0] + arrived_b[1] + arrived_b[2]
        return sum_a, sum_b

    rows_a, rows_b = reduced(part_a, x, 0, SIDE, part_b, z, 1, 1)
    mine_a, mine_b = reduced(rows_a, z, 0, 1, rows_b, x, 0, SIDE)
    mine = jnp.stack(
        [
            mine_a.reshape(SIDE, 2, ROWS, HALF),
            mine_b.reshape(SIDE, 2, ROWS, HALF),
        ],
        axis=2,
    ) * grad_scale
    kept = taken(mine, core, 1)
    came = exchanged(taken(mine, core ^ 1, 1), "group", 1)
    both = jnp.where(core == 0, jnp.stack([kept, came], 1), jnp.stack([came, kept], 1))
    blocks = [taken(both, y, 0)]
    for s in (1, 2, 3):
        blocks.append(exchanged(taken(both, y ^ s, 0), "group", 2 * s))
    sums, ordered = pl.pallas_call(
        gram_kernel,
        in_specs=[pl.BlockSpec(memory_space=pltpu.SMEM)] + in_vmem(SIDE),
        out_specs=in_vmem(2),
        out_shape=[
            jax.ShapeDtypeStruct((TOTAL, 128), jnp.float32),
            jax.ShapeDtypeStruct((GROUPS, 2, ROWS, HALF), jnp.float32),
        ],
        name="gram",
    )(y.reshape(1).astype(jnp.int32), *blocks)
    sums = lax.all_to_all(sums, ("blk", "group"), split_axis=0, concat_axis=0, tiled=True)
    return tuple(
        pl.pallas_call(
            finish_kernel,
            in_specs=in_vmem(4),
            out_specs=in_vmem(2),
            out_shape=[jax.ShapeDtypeStruct(weights.shape, jnp.float32)] * 2,
            name="finish",
        )(sums, ordered, weights, momentum)
    )


def solution(mesh):
    spec = P(("blk", "group"), None)
    return jax.shard_map(
        shards, mesh=mesh, in_specs=(spec,) * 4, out_specs=(spec,) * 2, check_vma=False
    )
```

```python
import functools
import math

import jax
import jax.numpy as jnp
from jax import lax
from jax.experimental import pallas as pl
from jax.experimental.pallas import tpu as pltpu
from jax.sharding import PartitionSpec as P

EPSILON = 1e-06
GROUPS = 8
SIDE = 4
ROWS = 16
COLS = 512
PIECE = GROUPS * ROWS
DEPTH = 1024
TOTAL = 128
CONTRACT = (((0,), (0,)), ((), ()))


def exchanged(value, axis, mask):
    return lax.ppermute(value, axis, [(k, k ^ mask) for k in range(lax.axis_size(axis))])


def in_vmem(count):
    return [pl.BlockSpec(memory_space=pltpu.VMEM)] * count


def piece_blocks(x, z, s):
    along_x = [(x ^ s) * SIDE + ((x ^ s) & 1) + 2 * k for k in range(2)]
    along_z = [((((z ^ s) & 1) ^ 1) + 2 * k) * SIDE + (z ^ s) for k in range(2)]
    return along_x + along_z


def product_kernel(masks, depth, added, place_ref, act_ref, out_ref, *refs):
    base_refs, refs = refs[: 2 * added], refs[2 * added :]
    pieces = refs[: 2 * len(masks)]
    held, grad, sems = refs[2 * len(masks) :]
    chunks = out_ref.shape[0] // depth
    blocks = [piece_blocks(place_ref[0], place_ref[1], s) for s in masks]

    def copies(k):
        rows = pl.ds(k * depth, depth)
        ends = [(out_ref.at[rows], grad.at[rows])]
        for n in range(len(masks)):
            for c in range(4):
                start = pl.multiple_of(blocks[n][c] * PIECE, PIECE)
                ends.append(
                    (act_ref.at[rows, pl.ds(start, PIECE)], held.at[n, rows, pl.ds(c * PIECE, PIECE)])
                )
        return [
            pltpu.make_async_copy(source, target, sems.at[k, place])
            for place, (source, target) in enumerate(ends)
        ]

    for k in range(chunks):
        for copy in copies(k):
            copy.start()
    for k in range(chunks):
        for copy in copies(k):
            copy.wait()
        rows = pl.ds(k * depth, depth)
        for n in range(len(masks)):
            part = lax.dot_general(
                held[n, rows], grad[rows], CONTRACT, preferred_element_type=jnp.float32
            )
            for way in range(2):
                piece = pieces[2 * n + way]
                mine = part[way * 2 * PIECE : (way + 1) * 2 * PIECE]
                if k:
                    piece[...] += mine
                elif added:
                    piece[...] = base_refs[way][...] + mine
                else:
                    piece[...] = mine


def products(activations, grad_out, place, masks, depth, vmem, base=()):
    tokens, cols = grad_out.shape
    count = 2 * len(masks)
    return pl.pallas_call(
        functools.partial(product_kernel, masks, depth, len(base) // 2),
        in_specs=[pl.BlockSpec(memory_space=pltpu.SMEM)]
        + [pl.BlockSpec(memory_space=pl.ANY)] * 2
        + in_vmem(len(base)),
        out_specs=in_vmem(count),
        out_shape=[jax.ShapeDtypeStruct((2 * PIECE, cols), jnp.float32)] * count,
        scratch_shapes=[
            pltpu.VMEM((len(masks), tokens, 4 * PIECE), activations.dtype),
            pltpu.VMEM((tokens, cols), grad_out.dtype),
            pltpu.SemaphoreType.DMA((tokens // depth, 1 + 4 * len(masks))),
        ],
        compiler_params=pltpu.CompilerParams(vmem_limit_bytes=vmem << 20),
        cost_estimate=pl.CostEstimate(flops=1000, bytes_accessed=1000, transcendentals=0),
        name="products",
    )(place, activations, grad_out, *base)


def pair_slots():
    return [(i, j) for i in range(GROUPS) for j in range(i, GROUPS)]


def gram_kernel(place_ref, *refs):
    *block_refs, sums_ref, ordered_ref = refs
    y = place_ref[0]
    slots = [[block_ref[core] for core in range(2)] for block_ref in block_refs]
    for bit in (1, 2):
        moved = (y & bit) != 0
        slots = [
            [jnp.where(moved, slots[k ^ bit][core], slots[k][core]) for core in range(2)]
            for k in range(SIDE)
        ]
    groups = [slots[i // 2][i % 2] for i in range(GROUPS)]
    for i in range(GROUPS):
        ordered_ref[i] = groups[i]
    rows = []
    for i, j in pair_slots():
        product = groups[i] * groups[j]
        product = product[:8] + product[8:]
        product = product[:, :256] + product[:, 256:]
        product = product[:, :128] + product[:, 128:]
        rows.append(jnp.sum(product, axis=0, keepdims=True))
    rows.append(jnp.zeros((128 - len(rows), 128), jnp.float32))
    sums_ref[...] = lax.dot_general(
        jnp.ones((TOTAL, 128), jnp.float32),
        jnp.concatenate(rows, axis=0),
        (((1,), (1,)), ((), ())),
        precision=lax.Precision.HIGHEST,
        preferred_element_type=jnp.float32,
    )


def finish_kernel(sums_ref, ordered_ref, weights_ref, momentum_ref, new_weights_ref, new_momentum_ref):
    sums = jnp.sum(sums_ref[...], axis=0, keepdims=True)
    gram = {}
    for place, (i, j) in enumerate(pair_slots()):
        gram[i, j] = gram[j, i] = sums[:, place : place + 1]
    shares = [1.0] * GROUPS
    count = GROUPS
    while count > 1:
        half = count // 2
        coef = [None] * count
        for i in range(half):
            cross = gram[i, i + half]
            coef[i] = 1.0 - cross / (2.0 * (jnp.maximum(gram[i, i], 0.0) + EPSILON))
            coef[i + half] = 1.0 - cross / (2.0 * (jnp.maximum(gram[i + half, i + half], 0.0) + EPSILON))
        shares = [shares[g] * coef[g % count] for g in range(GROUPS)]
        later = {}
        for i in range(half):
            for j in range(i, half):
                later[i, j] = later[j, i] = (
                    coef[i] * coef[j] * gram[i, j]
                    + coef[i + half] * coef[j + half] * gram[i + half, j + half]
                ) + (
                    coef[i] * coef[j + half] * gram[i, j + half]
                    + coef[i + half] * coef[j] * gram[i + half, j]
                )
        gram = later
        count = half
    combined = shares[0] * ordered_ref[0]
    for i in range(1, GROUPS):
        combined = combined + shares[i] * ordered_ref[i]
    new_momentum = 0.9 * momentum_ref[...] + combined
    new_momentum_ref[...] = new_momentum
    new_weights_ref[...] = (1.0 - 0.1 * 0.1) * weights_ref[...] - 0.1 * new_momentum


def second_pairs(s):
    pairs = []
    for k in range(SIDE * SIDE):
        x, z = k // SIDE, k % SIDE
        along_z = ((x ^ z) & 1 == 0) == (s == 2)
        pairs.append((k, k ^ s if along_z else k ^ (SIDE * s)))
    return pairs


def shards(activations, grad_out, weights, momentum):
    blk = lax.axis_index("blk")
    group = lax.axis_index("group")
    x, z = blk // SIDE, blk % SIDE
    y, core = group // 2, group % 2
    grad_scale = 1.0 / math.sqrt(activations.shape[0] * lax.axis_size("blk"))
    place = jnp.stack([x, z]).astype(jnp.int32)

    def taken(value, index, dim):
        return lax.dynamic_index_in_dim(value, index, dim, keepdims=False)

    def both_ways(pair, s):
        return [exchanged(pair[0], "blk", SIDE * s), exchanged(pair[1], "blk", s)]

    far = products(activations, grad_out, place, (2,), DEPTH, 62)
    far_came = both_ways(far, 2)
    place, far = lax.optimization_barrier((place, far))
    near = products(activations, grad_out, place, (1, 3), DEPTH, 50)
    near_came = both_ways(near[:2], 1), both_ways(near[2:], 3)
    place, near = lax.optimization_barrier((place, near))
    kept = products(activations, grad_out, place, (0,), DEPTH, 50, far_came)
    rows = jnp.concatenate(
        [own + a + b for own, a, b in zip(kept, *near_came)], axis=0
    ).reshape(4, PIECE, COLS)
    odd = (x ^ z) & 1
    mine = taken(rows, jnp.where(odd == 0, z >> 1, 2 + (x >> 1)), 0)
    for s in (2, 1, 3):
        if s == 2:
            sent = jnp.where(odd == 0, (z ^ 2) >> 1, 2 + ((x ^ 2) >> 1))
        else:
            sent = jnp.where(odd == 0, 2 + ((x ^ s) >> 1), (z ^ s) >> 1)
        mine = mine + lax.ppermute(taken(rows, sent, 0), "blk", second_pairs(s))
    mine = (mine * grad_scale).reshape(SIDE, 2, ROWS, COLS)
    kept = taken(mine, core, 1)
    came = exchanged(taken(mine, core ^ 1, 1), "group", 1)
    both = jnp.where(core == 0, jnp.stack([kept, came], 1), jnp.stack([came, kept], 1))
    blocks = [taken(both, y, 0)]
    for s in (1, 2, 3):
        blocks.append(exchanged(taken(both, y ^ s, 0), "group", 2 * s))
    sums, ordered = pl.pallas_call(
        gram_kernel,
        in_specs=[pl.BlockSpec(memory_space=pltpu.SMEM)] + in_vmem(SIDE),
        out_specs=in_vmem(2),
        out_shape=[
            jax.ShapeDtypeStruct((TOTAL, 128), jnp.float32),
            jax.ShapeDtypeStruct((GROUPS, ROWS, COLS), jnp.float32),
        ],
        compiler_params=pltpu.CompilerParams(vmem_limit_bytes=4 << 20),
        name="gram",
    )(y.reshape(1).astype(jnp.int32), *blocks)
    sums = lax.all_to_all(sums, ("blk", "group"), split_axis=0, concat_axis=0, tiled=True)
    return tuple(
        pl.pallas_call(
            finish_kernel,
            in_specs=in_vmem(4),
            out_specs=in_vmem(2),
            out_shape=[jax.ShapeDtypeStruct(weights.shape, jnp.float32)] * 2,
            compiler_params=pltpu.CompilerParams(vmem_limit_bytes=4 << 20),
            name="finish",
        )(sums, ordered, weights, momentum)
    )


def solution(mesh):
    spec = P(("blk", "group"), None)
    return jax.shard_map(
        shards, mesh=mesh, in_specs=(spec,) * 4, out_specs=(spec,) * 2, check_vma=False
    )
```

```python
import functools
import math

import jax
import jax.numpy as jnp
from jax import lax
from jax.experimental import pallas as pl
from jax.experimental.pallas import tpu as pltpu
from jax.sharding import PartitionSpec as P

EPSILON = 1e-06
GROUPS = 8
SIDE = 4
ROWS = 16
COLS = 512
PIECE = GROUPS * ROWS
DEPTH = 512
TOTAL = 128
CONTRACT = (((0,), (0,)), ((), ()))


def exchanged(value, axis, mask):
    return lax.ppermute(value, axis, [(k, k ^ mask) for k in range(lax.axis_size(axis))])


def in_vmem(count):
    return [pl.BlockSpec(memory_space=pltpu.VMEM)] * count


def my_place():
    blk, group = lax.axis_index("blk"), lax.axis_index("group")
    return blk // SIDE, blk % SIDE, group % 2


def piece_blocks(s):
    x, z, core = my_place()
    along_x = [(x ^ s) * SIDE + ((x ^ s ^ core) & 1) + 2 * k for k in range(2)]
    along_z = [(((z ^ s ^ core ^ 1) & 1) + 2 * k) * SIDE + (z ^ s) for k in range(2)]
    return along_x + along_z


def product_kernel(masks, depth, added, act_ref, out_ref, *refs):
    base_refs, refs = refs[: 2 * added], refs[2 * added :]
    pieces = refs[: 2 * len(masks)]
    held, grad, sems = refs[2 * len(masks) :]
    chunks = out_ref.shape[0] // depth
    blocks = [piece_blocks(s) for s in masks]

    def copies(k):
        rows = pl.ds(k * depth, depth)
        ends = [(out_ref.at[rows], grad.at[rows])]
        for n in range(len(masks)):
            for c in range(4):
                start = pl.multiple_of(blocks[n][c] * PIECE, PIECE)
                ends.append(
                    (act_ref.at[rows, pl.ds(start, PIECE)], held.at[n, rows, pl.ds(c * PIECE, PIECE)])
                )
        return [
            pltpu.make_async_copy(source, target, sems.at[k, place])
            for place, (source, target) in enumerate(ends)
        ]

    for k in range(chunks):
        for copy in copies(k):
            copy.start()
    for k in range(chunks):
        for copy in copies(k):
            copy.wait()
        rows = pl.ds(k * depth, depth)
        for n in range(len(masks)):
            part = lax.dot_general(
                held[n, rows], grad[rows], CONTRACT, preferred_element_type=jnp.float32
            )
            for way in range(2):
                piece = pieces[2 * n + way]
                mine = part[way * 2 * PIECE : (way + 1) * 2 * PIECE]
                if k:
                    piece[...] += mine
                elif added:
                    piece[...] = base_refs[way][...] + mine
                else:
                    piece[...] = mine


def products(activations, grad_out, masks, depth, vmem, base=()):
    tokens, cols = grad_out.shape
    count = 2 * len(masks)
    return pl.pallas_call(
        functools.partial(product_kernel, masks, depth, len(base) // 2),
        in_specs=[pl.BlockSpec(memory_space=pl.ANY)] * 2
        + in_vmem(len(base)),
        out_specs=in_vmem(count),
        out_shape=[jax.ShapeDtypeStruct((2 * PIECE, cols), jnp.float32)] * count,
        scratch_shapes=[
            pltpu.VMEM((len(masks), tokens, 4 * PIECE), activations.dtype),
            pltpu.VMEM((tokens, cols), grad_out.dtype),
            pltpu.SemaphoreType.DMA((tokens // depth, 1 + 4 * len(masks))),
        ],
        compiler_params=pltpu.CompilerParams(vmem_limit_bytes=vmem << 20),
        cost_estimate=pl.CostEstimate(flops=1000, bytes_accessed=1000, transcendentals=0),
        name="products",
    )(activations, grad_out, *base)


def summed_kernel(*refs):
    ways, out_refs = (refs[:3], refs[3:6]), refs[6:]
    x, z, core = my_place()
    along_x = ((x ^ z ^ core) & 1) == 1
    for out_ref, s in zip(out_refs, (0, 2, 1, 3)):
        from_first = jnp.logical_xor(along_x, s % 2 == 0)
        for way, place in enumerate((z ^ s, x ^ s)):

            @pl.when(from_first if way == 0 else jnp.logical_not(from_first))
            def _(way=way, place=place):
                rows = pl.ds(pl.multiple_of((place >> 1) * PIECE, PIECE), PIECE)
                own, one, three = ways[way]
                out_ref[...] = own[rows] + (one[rows] + three[rows])


def summed(kept, first, third):
    operands = [value for trio in zip(kept, first, third) for value in trio]
    return pl.pallas_call(
        summed_kernel,
        in_specs=in_vmem(6),
        out_specs=in_vmem(4),
        out_shape=[jax.ShapeDtypeStruct((PIECE, COLS), jnp.float32)] * 4,
        compiler_params=pltpu.CompilerParams(vmem_limit_bytes=8 << 20),
        name="summed",
    )(*operands)


def pair_slots():
    return [(i, j) for i in range(GROUPS) for j in range(i, GROUPS)]


def gram_kernel(place_ref, *refs):
    *block_refs, sums_ref, ordered_ref = refs
    y = place_ref[0]
    slots = [[block_ref[core] for core in range(2)] for block_ref in block_refs]
    for bit in (1, 2):
        moved = (y & bit) != 0
        slots = [
            [jnp.where(moved, slots[k ^ bit][core], slots[k][core]) for core in range(2)]
            for k in range(SIDE)
        ]
    groups = [slots[i // 2][i % 2] for i in range(GROUPS)]
    for i in range(GROUPS):
        ordered_ref[i] = groups[i]
    rows = []
    for i, j in pair_slots():
        product = groups[i] * groups[j]
        product = product[:8] + product[8:]
        product = product[:, :256] + product[:, 256:]
        product = product[:, :128] + product[:, 128:]
        rows.append(jnp.sum(product, axis=0, keepdims=True))
    rows.append(jnp.zeros((128 - len(rows), 128), jnp.float32))
    sums_ref[...] = lax.dot_general(
        jnp.ones((TOTAL, 128), jnp.float32),
        jnp.concatenate(rows, axis=0),
        (((1,), (1,)), ((), ())),
        precision=lax.Precision.HIGHEST,
        preferred_element_type=jnp.float32,
    )


def finish_kernel(sums_ref, ordered_ref, weights_ref, momentum_ref, new_weights_ref, new_momentum_ref):
    sums = jnp.sum(sums_ref[...], axis=0, keepdims=True)
    gram = {}
    for place, (i, j) in enumerate(pair_slots()):
        gram[i, j] = gram[j, i] = sums[:, place : place + 1]
    shares = [1.0] * GROUPS
    count = GROUPS
    while count > 1:
        half = count // 2
        coef = [None] * count
        for i in range(half):
            cross = gram[i, i + half]
            coef[i] = 1.0 - cross / (2.0 * (jnp.maximum(gram[i, i], 0.0) + EPSILON))
            coef[i + half] = 1.0 - cross / (2.0 * (jnp.maximum(gram[i + half, i + half], 0.0) + EPSILON))
        shares = [shares[g] * coef[g % count] for g in range(GROUPS)]
        later = {}
        for i in range(half):
            for j in range(i, half):
                later[i, j] = later[j, i] = (
                    coef[i] * coef[j] * gram[i, j]
                    + coef[i + half] * coef[j + half] * gram[i + half, j + half]
                ) + (
                    coef[i] * coef[j + half] * gram[i, j + half]
                    + coef[i + half] * coef[j] * gram[i + half, j]
                )
        gram = later
        count = half
    combined = shares[0] * ordered_ref[0]
    for i in range(1, GROUPS):
        combined = combined + shares[i] * ordered_ref[i]
    new_momentum = 0.9 * momentum_ref[...] + combined
    new_momentum_ref[...] = new_momentum
    new_weights_ref[...] = (1.0 - 0.1 * 0.1) * weights_ref[...] - 0.1 * new_momentum


def second_pairs(s):
    pairs = []
    for k in range(TOTAL):
        blk, core = k // GROUPS, k % 2
        along_z = ((blk // SIDE ^ blk ^ core) & 1 == 0) == (s == 2)
        pairs.append((k, k ^ (GROUPS * (s if along_z else SIDE * s))))
    return pairs


def shards(activations, grad_out, weights, momentum):
    group = lax.axis_index("group")
    y, core = group // 2, group % 2
    grad_scale = 1.0 / math.sqrt(activations.shape[0] * lax.axis_size("blk"))

    def taken(value, index, dim):
        return lax.dynamic_index_in_dim(value, index, dim, keepdims=False)

    def both_ways(pair, s):
        return [exchanged(pair[0], "blk", SIDE * s), exchanged(pair[1], "blk", s)]

    far = products(activations, grad_out, (2,), DEPTH, 62)
    far_came = both_ways(far, 2)
    grad_out, far = lax.optimization_barrier((grad_out, far))
    near = products(activations, grad_out, (1, 3), DEPTH, 50)
    near_came = both_ways(near[:2], 1), both_ways(near[2:], 3)
    grad_out, near = lax.optimization_barrier((grad_out, near))
    kept = products(activations, grad_out, (0,), DEPTH, 50, far_came)
    mine, *sent = summed(kept, *near_came)
    for value, s in zip(sent, (2, 1, 3)):
        mine = mine + lax.ppermute(value, ("blk", "group"), second_pairs(s))
    mine = (mine * grad_scale).reshape(SIDE, 2, ROWS, COLS)
    kept = taken(mine, core, 1)
    came = exchanged(taken(mine, core ^ 1, 1), "group", 1)
    both = jnp.where(core == 0, jnp.stack([kept, came], 1), jnp.stack([came, kept], 1))
    blocks = [taken(both, y, 0)]
    for s in (1, 2, 3):
        blocks.append(exchanged(taken(both, y ^ s, 0), "group", 2 * s))
    sums, ordered = pl.pallas_call(
        gram_kernel,
        in_specs=[pl.BlockSpec(memory_space=pltpu.SMEM)] + in_vmem(SIDE),
        out_specs=in_vmem(2),
        out_shape=[
            jax.ShapeDtypeStruct((TOTAL, 128), jnp.float32),
            jax.ShapeDtypeStruct((GROUPS, ROWS, COLS), jnp.float32),
        ],
        compiler_params=pltpu.CompilerParams(vmem_limit_bytes=4 << 20),
        name="gram",
    )(y.reshape(1).astype(jnp.int32), *blocks)
    sums = lax.all_to_all(sums, ("blk", "group"), split_axis=0, concat_axis=0, tiled=True)
    return tuple(
        pl.pallas_call(
            finish_kernel,
            in_specs=in_vmem(4),
            out_specs=in_vmem(2),
            out_shape=[jax.ShapeDtypeStruct(weights.shape, jnp.float32)] * 2,
            compiler_params=pltpu.CompilerParams(vmem_limit_bytes=4 << 20),
            name="finish",
        )(sums, ordered, weights, momentum)
    )


def solution(mesh):
    spec = P(("blk", "group"), None)
    return jax.shard_map(
        shards, mesh=mesh, in_specs=(spec,) * 4, out_specs=(spec,) * 2, check_vma=False
    )
```

```python
import functools
import math

import jax
import jax.numpy as jnp
from jax import lax
from jax.experimental import pallas as pl
from jax.experimental.pallas import tpu as pltpu
from jax.sharding import PartitionSpec as P

EPSILON = 1e-06
GROUPS = 8
SIDE = 4
ROWS = 16
COLS = 512
PIECE = GROUPS * ROWS
DEPTH = 512
ORDER = (2, 1, 3)
TOTAL = 128
CONTRACT = (((0,), (0,)), ((), ()))


def exchanged(value, axis, mask):
    return lax.ppermute(value, axis, [(k, k ^ mask) for k in range(lax.axis_size(axis))])


def in_vmem(count):
    return [pl.BlockSpec(memory_space=pltpu.VMEM)] * count


def my_place():
    blk, core = lax.axis_index("blk"), lax.axis_index("group") % 2
    x, z = blk // SIDE, blk % SIDE
    return jnp.where(core == 0, x, z), jnp.where(core == 0, z, x), core


def piece_blocks(units):
    first, _, core = my_place()
    return [
        jnp.where(core == 0, (first ^ s) * SIDE + k, k * SIDE + (first ^ s))
        for s, h in units
        for k in (2 * h, 2 * h + 1)
    ]


def way_pairs(s, half):
    along_x = [core == half for core in range(2)]
    return [
        (k, k ^ (GROUPS * s * (SIDE if along_x[k % 2] else 1))) for k in range(TOTAL)
    ]


def sent_over(value, s, half):
    return lax.ppermute(value, ("blk", "group"), way_pairs(s, half))


def product_kernel(units, depth, act_ref, out_ref, *refs):
    *refs, held, grad, sems = refs
    pieces, base = refs[-len(units) :], refs[: -len(units)]
    chunks = out_ref.shape[0] // depth
    blocks = piece_blocks(units)

    def copies(k):
        rows = pl.ds(k * depth, depth)
        ends = [(out_ref.at[rows], grad.at[rows])]
        for c, block in enumerate(blocks):
            start = pl.multiple_of(block * PIECE, PIECE)
            ends.append(
                (act_ref.at[rows, pl.ds(start, PIECE)], held.at[rows, pl.ds(c * PIECE, PIECE)])
            )
        return [
            pltpu.make_async_copy(source, target, sems.at[k, place])
            for place, (source, target) in enumerate(ends)
        ]

    for k in range(chunks):
        for copy in copies(k):
            copy.start()
    for k in range(chunks):
        for copy in copies(k):
            copy.wait()
        rows = pl.ds(k * depth, depth)
        part = lax.dot_general(held[rows], grad[rows], CONTRACT, preferred_element_type=jnp.float32)
        for n, piece in enumerate(pieces):
            mine = part[n * 2 * PIECE : (n + 1) * 2 * PIECE]
            if k:
                piece[...] += mine
            elif base:
                piece[...] = base[n][...] + mine
            else:
                piece[...] = mine


def products(activations, grad_out, units, vmem, base=()):
    tokens, cols = grad_out.shape
    return pl.pallas_call(
        functools.partial(product_kernel, units, DEPTH),
        in_specs=[pl.BlockSpec(memory_space=pl.ANY)] * 2 + in_vmem(len(base)),
        out_specs=in_vmem(len(units)),
        out_shape=[jax.ShapeDtypeStruct((2 * PIECE, cols), jnp.float32)] * len(units),
        scratch_shapes=[
            pltpu.VMEM((tokens, 2 * PIECE * len(units)), activations.dtype),
            pltpu.VMEM((tokens, cols), grad_out.dtype),
            pltpu.SemaphoreType.DMA((tokens // DEPTH, 1 + 2 * len(units))),
        ],
        compiler_params=pltpu.CompilerParams(vmem_limit_bytes=vmem << 20),
        cost_estimate=pl.CostEstimate(flops=1000, bytes_accessed=1000, transcendentals=0),
        name="products",
    )(activations, grad_out, *base)


def summed_kernel(own_lower_ref, own_upper_ref, lower_ref, upper_ref, *out_refs):
    _, second, _ = my_place()
    for out_ref, s in zip(out_refs, (0, *ORDER)):
        place = second ^ s
        rows = pl.ds(pl.multiple_of((place & 1) * PIECE, PIECE), PIECE)

        @pl.when(place < 2)
        def _():
            out_ref[...] = own_lower_ref[rows] + lower_ref[rows]

        @pl.when(place >= 2)
        def _():
            out_ref[...] = own_upper_ref[rows] + upper_ref[rows]


def summed(*values):
    return pl.pallas_call(
        summed_kernel,
        in_specs=in_vmem(4),
        out_specs=in_vmem(4),
        out_shape=[jax.ShapeDtypeStruct((PIECE, COLS), jnp.float32)] * 4,
        compiler_params=pltpu.CompilerParams(vmem_limit_bytes=8 << 20),
        name="summed",
    )(*values)


def pair_slots():
    return [(i, j) for i in range(GROUPS) for j in range(i, GROUPS)]


def gram_kernel(place_ref, *refs):
    *block_refs, sums_ref, ordered_ref = refs
    y = place_ref[0]
    slots = [[block_ref[core] for core in range(2)] for block_ref in block_refs]
    for bit in (1, 2):
        moved = (y & bit) != 0
        slots = [
            [jnp.where(moved, slots[k ^ bit][core], slots[k][core]) for core in range(2)]
            for k in range(SIDE)
        ]
    groups = [slots[i // 2][i % 2] for i in range(GROUPS)]
    for i in range(GROUPS):
        ordered_ref[i] = groups[i]
    rows = []
    for i, j in pair_slots():
        product = groups[i] * groups[j]
        product = product[:8] + product[8:]
        product = product[:, :256] + product[:, 256:]
        product = product[:, :128] + product[:, 128:]
        rows.append(jnp.sum(product, axis=0, keepdims=True))
    rows.append(jnp.zeros((128 - len(rows), 128), jnp.float32))
    sums_ref[...] = lax.dot_general(
        jnp.ones((TOTAL, 128), jnp.float32),
        jnp.concatenate(rows, axis=0),
        (((1,), (1,)), ((), ())),
        precision=lax.Precision.HIGHEST,
        preferred_element_type=jnp.float32,
    )


def finish_kernel(sums_ref, ordered_ref, weights_ref, momentum_ref, new_weights_ref, new_momentum_ref):
    sums = jnp.sum(sums_ref[...], axis=0, keepdims=True)
    gram = {}
    for place, (i, j) in enumerate(pair_slots()):
        gram[i, j] = gram[j, i] = sums[:, place : place + 1]
    shares = [1.0] * GROUPS
    count = GROUPS
    while count > 1:
        half = count // 2
        coef = [None] * count
        for i in range(half):
            cross = gram[i, i + half]
            coef[i] = 1.0 - cross / (2.0 * (jnp.maximum(gram[i, i], 0.0) + EPSILON))
            coef[i + half] = 1.0 - cross / (2.0 * (jnp.maximum(gram[i + half, i + half], 0.0) + EPSILON))
        shares = [shares[g] * coef[g % count] for g in range(GROUPS)]
        later = {}
        for i in range(half):
            for j in range(i, half):
                later[i, j] = later[j, i] = (
                    coef[i] * coef[j] * gram[i, j]
                    + coef[i + half] * coef[j + half] * gram[i + half, j + half]
                ) + (
                    coef[i] * coef[j + half] * gram[i, j + half]
                    + coef[i + half] * coef[j] * gram[i + half, j]
                )
        gram = later
        count = half
    combined = shares[0] * ordered_ref[0]
    for i in range(1, GROUPS):
        combined = combined + shares[i] * ordered_ref[i]
    new_momentum = 0.9 * momentum_ref[...] + combined
    new_momentum_ref[...] = new_momentum
    new_weights_ref[...] = (1.0 - 0.1 * 0.1) * weights_ref[...] - 0.1 * new_momentum


def shards(activations, grad_out, weights, momentum):
    group = lax.axis_index("group")
    y, core = group // 2, group % 2
    grad_scale = 1.0 / math.sqrt(activations.shape[0] * lax.axis_size("blk"))

    def taken(value, index, dim):
        return lax.dynamic_index_in_dim(value, index, dim, keepdims=False)

    def ordered(pair):
        nonlocal grad_out
        grad_out, pair = lax.optimization_barrier((grad_out, pair))
        return pair

    def to_neighbours(pair):
        return sent_over(pair[0], 1, 0), sent_over(pair[1], 3, 0)

    far = ordered(products(activations, grad_out, ((2, 0), (2, 1)), 60))
    lower, upper = to_neighbours(far)
    direct = ordered(products(activations, grad_out, ((1, 0), (3, 1)), 50))
    direct_came = to_neighbours(direct)
    passed = ordered(products(activations, grad_out, ((1, 1), (3, 0)), 50, (upper, lower)))
    upper, lower = to_neighbours(passed)
    kept = products(activations, grad_out, ((0, 0), (0, 1)), 50, direct_came)
    mine, *sent = summed(*kept, lower, upper)
    for value, s in zip(sent, ORDER):
        mine = mine + sent_over(value, s, 1)
    mine = (mine * grad_scale).reshape(SIDE, 2, ROWS, COLS)
    kept = taken(mine, core, 1)
    came = exchanged(taken(mine, core ^ 1, 1), "group", 1)
    both = jnp.where(core == 0, jnp.stack([kept, came], 1), jnp.stack([came, kept], 1))
    blocks = [taken(both, y, 0)]
    for s in (1, 2, 3):
        blocks.append(exchanged(taken(both, y ^ s, 0), "group", 2 * s))
    sums, ordered = pl.pallas_call(
        gram_kernel,
        in_specs=[pl.BlockSpec(memory_space=pltpu.SMEM)] + in_vmem(SIDE),
        out_specs=in_vmem(2),
        out_shape=[
            jax.ShapeDtypeStruct((TOTAL, 128), jnp.float32),
            jax.ShapeDtypeStruct((GROUPS, ROWS, COLS), jnp.float32),
        ],
        compiler_params=pltpu.CompilerParams(vmem_limit_bytes=4 << 20),
        name="gram",
    )(y.reshape(1).astype(jnp.int32), *blocks)
    sums = lax.all_to_all(sums, ("blk", "group"), split_axis=0, concat_axis=0, tiled=True)
    return tuple(
        pl.pallas_call(
            finish_kernel,
            in_specs=in_vmem(4),
            out_specs=in_vmem(2),
            out_shape=[jax.ShapeDtypeStruct(weights.shape, jnp.float32)] * 2,
            compiler_params=pltpu.CompilerParams(vmem_limit_bytes=4 << 20),
            name="finish",
        )(sums, ordered, weights, momentum)
    )


def solution(mesh):
    spec = P(("blk", "group"), None)
    return jax.shard_map(
        shards, mesh=mesh, in_specs=(spec,) * 4, out_specs=(spec,) * 2, check_vma=False
    )
```

```python
import functools
import math

import jax
import jax.numpy as jnp
from jax import lax
from jax.experimental import pallas as pl
from jax.experimental.pallas import tpu as pltpu
from jax.sharding import PartitionSpec as P

EPSILON = 1e-06
GROUPS = 8
SIDE = 4
ROWS = 16
COLS = 512
PIECE = GROUPS * ROWS
DEPTH = 512
ORDER = (2, 1, 3)
TOTAL = 128
CONTRACT = (((0,), (0,)), ((), ()))


def exchanged(value, axis, mask):
    return lax.ppermute(value, axis, [(k, k ^ mask) for k in range(lax.axis_size(axis))])


def in_vmem(count):
    return [pl.BlockSpec(memory_space=pltpu.VMEM)] * count


def my_place():
    blk, core = lax.axis_index("blk"), lax.axis_index("group") % 2
    x, z = blk // SIDE, blk % SIDE
    return jnp.where(core == 0, x, z), jnp.where(core == 0, z, x), core


def piece_blocks(units):
    first, _, core = my_place()
    return [
        jnp.where(core == 0, (first ^ s) * SIDE + k, k * SIDE + (first ^ s))
        for s, h in units
        for k in (2 * h, 2 * h + 1)
    ]


def way_pairs(s, half):
    along_x = [core == half for core in range(2)]
    return [
        (k, k ^ (GROUPS * s * (SIDE if along_x[k % 2] else 1))) for k in range(TOTAL)
    ]


def sent_over(value, s, half):
    return lax.ppermute(value, ("blk", "group"), way_pairs(s, half))


def product_kernel(units, later, held_ready, grad_ready, based, *refs):
    refs = list(refs)
    act_ref, out_ref = refs.pop(0), refs.pop(0)
    held = refs.pop(0) if held_ready else None
    base = [refs.pop(0) for _ in units] if based else ()
    pieces = [refs.pop(0) for _ in units]
    grad = out_ref if grad_ready else refs.pop(0)
    later_held = refs.pop(0) if later else None
    held = held if held_ready else refs.pop(0)
    tokens = grad.shape[0]
    chunks = tokens // DEPTH

    def block_copies(units, held, k):
        rows = pl.ds(k * DEPTH, DEPTH)
        ends = []
        for c, block in enumerate(piece_blocks(units)):
            columns = pl.ds(pl.multiple_of(block * PIECE, PIECE), PIECE)
            ends.append((act_ref.at[rows, columns], held.at[rows, pl.ds(c * PIECE, PIECE)]))
        return ends

    def started(ends, k):
        copies = [
            pltpu.make_async_copy(source, target, refs[0].at[k, place])
            for place, (source, target) in enumerate(ends)
        ]
        for copy in copies:
            copy.start()
        return copies

    copies = []
    for k in range(chunks):
        rows = pl.ds(k * DEPTH, DEPTH)
        ends = [] if held_ready else block_copies(units, held, k)
        if not grad_ready:
            ends.append((out_ref.at[rows], grad.at[rows]))
        copies.append(started(ends, k) if ends else [])
    if later:
        for k in range(chunks):
            copies.append(started(block_copies(later, later_held, k), chunks + k))
    for k in range(chunks):
        for copy in copies[k]:
            copy.wait()
        rows = pl.ds(k * DEPTH, DEPTH)
        part = lax.dot_general(held[rows], grad[rows], CONTRACT, preferred_element_type=jnp.float32)
        for n, piece in enumerate(pieces):
            mine = part[n * 2 * PIECE : (n + 1) * 2 * PIECE]
            if k:
                piece[...] += mine
            elif based:
                piece[...] = base[n][...] + mine
            else:
                piece[...] = mine
    for chunk in copies[chunks:]:
        for copy in chunk:
            copy.wait()


def products(activations, grad_out, units, later=(), held=None, grad_ready=True, base=()):
    tokens, cols = grad_out.shape
    wide = jax.ShapeDtypeStruct((tokens, 2 * PIECE * len(units)), activations.dtype)
    flat = jax.ShapeDtypeStruct((tokens, cols), grad_out.dtype)
    chunks = tokens // DEPTH * (2 if later else 1)
    scratch = [] if held is not None else [pltpu.VMEM(wide.shape, wide.dtype)]
    scratch.append(pltpu.SemaphoreType.DMA((chunks, 1 + 2 * len(units))))

    def placed(value, ready):
        return pltpu.with_memory_space_constraint(value, pltpu.VMEM if ready else pltpu.HBM)

    def spec(ready):
        return pl.BlockSpec(memory_space=pltpu.VMEM if ready else pl.ANY)

    ready = [] if held is None else [placed(held, True)]
    outs = [jax.ShapeDtypeStruct((2 * PIECE, cols), jnp.float32)] * len(units)
    outs += ([] if grad_ready else [flat]) + ([wide] if later else [])
    return pl.pallas_call(
        functools.partial(product_kernel, units, later, held is not None, grad_ready, bool(base)),
        in_specs=[spec(False), spec(grad_ready)] + in_vmem(len(ready) + len(base)),
        out_specs=in_vmem(len(outs)),
        out_shape=outs,
        scratch_shapes=scratch,
        compiler_params=pltpu.CompilerParams(vmem_limit_bytes=24 << 20),
        cost_estimate=pl.CostEstimate(flops=1000, bytes_accessed=1000, transcendentals=0),
        name="products",
    )(placed(activations, False), placed(grad_out, grad_ready), *ready, *base)


def relayed_kernel(*refs):
    for one_ref, other_ref, out_ref in zip(refs[:2], refs[2:4], refs[4:]):
        out_ref[...] = one_ref[...] + other_ref[...]


def relayed(own, came):
    return pl.pallas_call(
        relayed_kernel,
        in_specs=in_vmem(4),
        out_specs=in_vmem(2),
        out_shape=[jax.ShapeDtypeStruct(value.shape, value.dtype) for value in own],
        compiler_params=pltpu.CompilerParams(vmem_limit_bytes=8 << 20),
        cost_estimate=pl.CostEstimate(flops=1000, bytes_accessed=1000, transcendentals=0),
        name="relayed",
    )(*own, *came)


def summed_kernel(own_lower_ref, own_upper_ref, lower_ref, upper_ref, *out_refs):
    _, second, _ = my_place()
    for out_ref, s in zip(out_refs, (0, *ORDER)):
        place = second ^ s
        rows = pl.ds(pl.multiple_of((place & 1) * PIECE, PIECE), PIECE)

        @pl.when(place < 2)
        def _():
            out_ref[...] = own_lower_ref[rows] + lower_ref[rows]

        @pl.when(place >= 2)
        def _():
            out_ref[...] = own_upper_ref[rows] + upper_ref[rows]


def summed(*values):
    return pl.pallas_call(
        summed_kernel,
        in_specs=in_vmem(4),
        out_specs=in_vmem(4),
        out_shape=[jax.ShapeDtypeStruct((PIECE, COLS), jnp.float32)] * 4,
        compiler_params=pltpu.CompilerParams(vmem_limit_bytes=8 << 20),
        name="summed",
    )(*values)


def pair_slots():
    return [(i, j) for i in range(GROUPS) for j in range(i, GROUPS)]


def gram_kernel(place_ref, *refs):
    *block_refs, sums_ref, ordered_ref = refs
    y = place_ref[0]
    slots = [[block_ref[core] for core in range(2)] for block_ref in block_refs]
    for bit in (1, 2):
        moved = (y & bit) != 0
        slots = [
            [jnp.where(moved, slots[k ^ bit][core], slots[k][core]) for core in range(2)]
            for k in range(SIDE)
        ]
    groups = [slots[i // 2][i % 2] for i in range(GROUPS)]
    for i in range(GROUPS):
        ordered_ref[i] = groups[i]
    rows = []
    for i, j in pair_slots():
        product = groups[i] * groups[j]
        product = product[:8] + product[8:]
        product = product[:, :256] + product[:, 256:]
        product = product[:, :128] + product[:, 128:]
        rows.append(jnp.sum(product, axis=0, keepdims=True))
    rows.append(jnp.zeros((128 - len(rows), 128), jnp.float32))
    sums_ref[...] = lax.dot_general(
        jnp.ones((TOTAL, 128), jnp.float32),
        jnp.concatenate(rows, axis=0),
        (((1,), (1,)), ((), ())),
        precision=lax.Precision.HIGHEST,
        preferred_element_type=jnp.float32,
    )


def finish_kernel(sums_ref, ordered_ref, weights_ref, momentum_ref, new_weights_ref, new_momentum_ref):
    sums = jnp.sum(sums_ref[...], axis=0, keepdims=True)
    gram = {}
    for place, (i, j) in enumerate(pair_slots()):
        gram[i, j] = gram[j, i] = sums[:, place : place + 1]
    shares = [1.0] * GROUPS
    count = GROUPS
    while count > 1:
        half = count // 2
        coef = [None] * count
        for i in range(half):
            cross = gram[i, i + half]
            coef[i] = 1.0 - cross / (2.0 * (jnp.maximum(gram[i, i], 0.0) + EPSILON))
            coef[i + half] = 1.0 - cross / (2.0 * (jnp.maximum(gram[i + half, i + half], 0.0) + EPSILON))
        shares = [shares[g] * coef[g % count] for g in range(GROUPS)]
        later = {}
        for i in range(half):
            for j in range(i, half):
                later[i, j] = later[j, i] = (
                    coef[i] * coef[j] * gram[i, j]
                    + coef[i + half] * coef[j + half] * gram[i + half, j + half]
                ) + (
                    coef[i] * coef[j + half] * gram[i, j + half]
                    + coef[i + half] * coef[j] * gram[i + half, j]
                )
        gram = later
        count = half
    combined = shares[0] * ordered_ref[0]
    for i in range(1, GROUPS):
        combined = combined + shares[i] * ordered_ref[i]
    new_momentum = 0.9 * momentum_ref[...] + combined
    new_momentum_ref[...] = new_momentum
    new_weights_ref[...] = (1.0 - 0.1 * 0.1) * weights_ref[...] - 0.1 * new_momentum


def shards(activations, grad_out, weights, momentum):
    group = lax.axis_index("group")
    y, core = group // 2, group % 2
    grad_scale = 1.0 / math.sqrt(activations.shape[0] * lax.axis_size("blk"))

    def taken(value, index, dim):
        return lax.dynamic_index_in_dim(value, index, dim, keepdims=False)

    def to_neighbours(pair):
        return sent_over(pair[0], 1, 0), sent_over(pair[1], 3, 0)

    after, own = ((1, 1), (3, 0)), ((0, 0), (0, 1))
    *far, grad = products(activations, grad_out, ((2, 0), (2, 1)), grad_ready=False)
    lower, upper = to_neighbours(far)
    *direct, held = products(activations, grad, ((1, 0), (3, 1)), later=after)
    direct_came = to_neighbours(direct)
    *passed, held = products(activations, grad, after, later=own, held=held)
    upper, lower = to_neighbours(relayed(passed, (upper, lower)))
    kept = products(activations, grad, own, held=held, base=direct_came)
    mine, *sent = summed(*kept, lower, upper)
    for value, s in zip(sent, ORDER):
        mine = mine + sent_over(value, s, 1)
    mine = (mine * grad_scale).reshape(SIDE, 2, ROWS, COLS)
    kept = taken(mine, core, 1)
    came = exchanged(taken(mine, core ^ 1, 1), "group", 1)
    both = jnp.where(core == 0, jnp.stack([kept, came], 1), jnp.stack([came, kept], 1))
    blocks = [taken(both, y, 0)]
    for s in (1, 2, 3):
        blocks.append(exchanged(taken(both, y ^ s, 0), "group", 2 * s))
    sums, ordered = pl.pallas_call(
        gram_kernel,
        in_specs=[pl.BlockSpec(memory_space=pltpu.SMEM)] + in_vmem(SIDE),
        out_specs=in_vmem(2),
        out_shape=[
            jax.ShapeDtypeStruct((TOTAL, 128), jnp.float32),
            jax.ShapeDtypeStruct((GROUPS, ROWS, COLS), jnp.float32),
        ],
        compiler_params=pltpu.CompilerParams(vmem_limit_bytes=4 << 20),
        name="gram",
    )(y.reshape(1).astype(jnp.int32), *blocks)
    sums = lax.all_to_all(sums, ("blk", "group"), split_axis=0, concat_axis=0, tiled=True)
    return tuple(
        pl.pallas_call(
            finish_kernel,
            in_specs=in_vmem(4),
            out_specs=in_vmem(2),
            out_shape=[jax.ShapeDtypeStruct(weights.shape, jnp.float32)] * 2,
            compiler_params=pltpu.CompilerParams(vmem_limit_bytes=4 << 20),
            name="finish",
        )(sums, ordered, weights, momentum)
    )


def solution(mesh):
    spec = P(("blk", "group"), None)
    return jax.shard_map(
        shards, mesh=mesh, in_specs=(spec,) * 4, out_specs=(spec,) * 2, check_vma=False
    )
```

```python
import functools
import math

import jax
import jax.numpy as jnp
from jax import lax
from jax.experimental import pallas as pl
from jax.experimental.pallas import tpu as pltpu
from jax.sharding import PartitionSpec as P

EPSILON = 1e-06
GROUPS = 8
SIDE = 4
ROWS = 16
COLS = 512
PIECE = GROUPS * ROWS
DEPTH = 512
ORDER = (2, 1, 3)
TOTAL = 128
CONTRACT = (((0,), (0,)), ((), ()))


def exchanged(value, axis, mask):
    return lax.ppermute(value, axis, [(k, k ^ mask) for k in range(lax.axis_size(axis))])


def in_vmem(count):
    return [pl.BlockSpec(memory_space=pltpu.VMEM)] * count


def my_place():
    blk, core = lax.axis_index("blk"), lax.axis_index("group") % 2
    x, z = blk // SIDE, blk % SIDE
    return jnp.where(core == 0, x, z), jnp.where(core == 0, z, x), core


def piece_blocks(units):
    first, _, core = my_place()
    return [
        jnp.where(core == 0, (first ^ s) * SIDE + k, k * SIDE + (first ^ s))
        for s, h in units
        for k in (2 * h, 2 * h + 1)
    ]


def way_pairs(s, half):
    along_x = [core == half for core in range(2)]
    return [
        (k, k ^ (GROUPS * s * (SIDE if along_x[k % 2] else 1))) for k in range(TOTAL)
    ]


def sent_over(value, s, half):
    return lax.ppermute(value, ("blk", "group"), way_pairs(s, half))


def product_kernel(units, grad_ready, based, *refs):
    refs = list(refs)
    act_ref, out_ref = refs.pop(0), refs.pop(0)
    base = [refs.pop(0) for _ in units] if based else ()
    pieces = [refs.pop(0) for _ in units]
    grad = out_ref if grad_ready else refs.pop(0)
    held, sems = refs
    chunks = grad.shape[0] // DEPTH
    blocks = piece_blocks(units)
    copies = []
    for k in range(chunks):
        rows = pl.ds(k * DEPTH, DEPTH)
        ends = [] if grad_ready else [(out_ref.at[rows], grad.at[rows])]
        for c, block in enumerate(blocks):
            columns = pl.ds(pl.multiple_of(block * PIECE, PIECE), PIECE)
            ends.append((act_ref.at[rows, columns], held.at[rows, pl.ds(c * PIECE, PIECE)]))
        copies.append(
            [
                pltpu.make_async_copy(source, target, sems.at[k, place])
                for place, (source, target) in enumerate(ends)
            ]
        )
        for copy in copies[k]:
            copy.start()
    for k in range(chunks):
        for copy in copies[k]:
            copy.wait()
        rows = pl.ds(k * DEPTH, DEPTH)
        part = lax.dot_general(held[rows], grad[rows], CONTRACT, preferred_element_type=jnp.float32)
        for n, piece in enumerate(pieces):
            mine = part[n * 2 * PIECE : (n + 1) * 2 * PIECE]
            if k:
                piece[...] += mine
            elif based:
                piece[...] = base[n][...] + mine
            else:
                piece[...] = mine


def products(activations, grad_out, units, grad_ready=True, base=()):
    tokens, cols = grad_out.shape
    flat = jax.ShapeDtypeStruct((tokens, cols), grad_out.dtype)
    outs = [jax.ShapeDtypeStruct((2 * PIECE, cols), jnp.float32)] * len(units)
    outs += [] if grad_ready else [flat]
    out_space = pltpu.VMEM if grad_ready else pltpu.HBM
    return pl.pallas_call(
        functools.partial(product_kernel, units, grad_ready, bool(base)),
        in_specs=[
            pl.BlockSpec(memory_space=pl.ANY),
            pl.BlockSpec(memory_space=pltpu.VMEM if grad_ready else pl.ANY),
        ]
        + in_vmem(len(base)),
        out_specs=in_vmem(len(outs)),
        out_shape=outs,
        scratch_shapes=[
            pltpu.VMEM((tokens, 2 * PIECE * len(units)), activations.dtype),
            pltpu.SemaphoreType.DMA((tokens // DEPTH, 1 + 2 * len(units))),
        ],
        compiler_params=pltpu.CompilerParams(vmem_limit_bytes=24 << 20),
        cost_estimate=pl.CostEstimate(flops=1000, bytes_accessed=1000, transcendentals=0),
        name="products",
    )(
        pltpu.with_memory_space_constraint(activations, pltpu.HBM),
        pltpu.with_memory_space_constraint(grad_out, out_space),
        *base,
    )


def relayed_kernel(*refs):
    for one_ref, other_ref, out_ref in zip(refs[:2], refs[2:4], refs[4:]):
        out_ref[...] = one_ref[...] + other_ref[...]


def relayed(own, came):
    return pl.pallas_call(
        relayed_kernel,
        in_specs=in_vmem(4),
        out_specs=in_vmem(2),
        out_shape=[jax.ShapeDtypeStruct(value.shape, value.dtype) for value in own],
        compiler_params=pltpu.CompilerParams(vmem_limit_bytes=8 << 20),
        cost_estimate=pl.CostEstimate(flops=1000, bytes_accessed=1000, transcendentals=0),
        name="relayed",
    )(*own, *came)


def summed_kernel(own_lower_ref, own_upper_ref, lower_ref, upper_ref, *out_refs):
    _, second, _ = my_place()
    for out_ref, s in zip(out_refs, (0, *ORDER)):
        place = second ^ s
        rows = pl.ds(pl.multiple_of((place & 1) * PIECE, PIECE), PIECE)

        @pl.when(place < 2)
        def _():
            out_ref[...] = own_lower_ref[rows] + lower_ref[rows]

        @pl.when(place >= 2)
        def _():
            out_ref[...] = own_upper_ref[rows] + upper_ref[rows]


def summed(*values):
    return pl.pallas_call(
        summed_kernel,
        in_specs=in_vmem(4),
        out_specs=in_vmem(4),
        out_shape=[jax.ShapeDtypeStruct((PIECE, COLS), jnp.float32)] * 4,
        compiler_params=pltpu.CompilerParams(vmem_limit_bytes=8 << 20),
        name="summed",
    )(*values)


def pair_slots():
    return [(i, j) for i in range(GROUPS) for j in range(i, GROUPS)]


def gram_kernel(place_ref, *refs):
    *block_refs, sums_ref, ordered_ref = refs
    y = place_ref[0]
    slots = [[block_ref[core] for core in range(2)] for block_ref in block_refs]
    for bit in (1, 2):
        moved = (y & bit) != 0
        slots = [
            [jnp.where(moved, slots[k ^ bit][core], slots[k][core]) for core in range(2)]
            for k in range(SIDE)
        ]
    groups = [slots[i // 2][i % 2] for i in range(GROUPS)]
    for i in range(GROUPS):
        ordered_ref[i] = groups[i]
    rows = []
    for i, j in pair_slots():
        product = groups[i] * groups[j]
        product = product[:8] + product[8:]
        product = product[:, :256] + product[:, 256:]
        product = product[:, :128] + product[:, 128:]
        rows.append(jnp.sum(product, axis=0, keepdims=True))
    rows.append(jnp.zeros((128 - len(rows), 128), jnp.float32))
    sums_ref[...] = lax.dot_general(
        jnp.ones((TOTAL, 128), jnp.float32),
        jnp.concatenate(rows, axis=0),
        (((1,), (1,)), ((), ())),
        precision=lax.Precision.HIGHEST,
        preferred_element_type=jnp.float32,
    )


def finish_kernel(sums_ref, ordered_ref, weights_ref, momentum_ref, new_weights_ref, new_momentum_ref):
    sums = jnp.sum(sums_ref[...], axis=0, keepdims=True)
    gram = {}
    for place, (i, j) in enumerate(pair_slots()):
        gram[i, j] = gram[j, i] = sums[:, place : place + 1]
    shares = [1.0] * GROUPS
    count = GROUPS
    while count > 1:
        half = count // 2
        coef = [None] * count
        for i in range(half):
            cross = gram[i, i + half]
            coef[i] = 1.0 - cross / (2.0 * (jnp.maximum(gram[i, i], 0.0) + EPSILON))
            coef[i + half] = 1.0 - cross / (2.0 * (jnp.maximum(gram[i + half, i + half], 0.0) + EPSILON))
        shares = [shares[g] * coef[g % count] for g in range(GROUPS)]
        later = {}
        for i in range(half):
            for j in range(i, half):
                later[i, j] = later[j, i] = (
                    coef[i] * coef[j] * gram[i, j]
                    + coef[i + half] * coef[j + half] * gram[i + half, j + half]
                ) + (
                    coef[i] * coef[j + half] * gram[i, j + half]
                    + coef[i + half] * coef[j] * gram[i + half, j]
                )
        gram = later
        count = half
    combined = shares[0] * ordered_ref[0]
    for i in range(1, GROUPS):
        combined = combined + shares[i] * ordered_ref[i]
    new_momentum = 0.9 * momentum_ref[...] + combined
    new_momentum_ref[...] = new_momentum
    new_weights_ref[...] = (1.0 - 0.1 * 0.1) * weights_ref[...] - 0.1 * new_momentum


def shards(activations, grad_out, weights, momentum):
    group = lax.axis_index("group")
    y, core = group // 2, group % 2
    grad_scale = 1.0 / math.sqrt(activations.shape[0] * lax.axis_size("blk"))

    def taken(value, index, dim):
        return lax.dynamic_index_in_dim(value, index, dim, keepdims=False)

    def to_neighbours(pair):
        return sent_over(pair[0], 1, 0), sent_over(pair[1], 3, 0)

    after, own = ((1, 1), (3, 0)), ((0, 0), (0, 1))
    *far, grad = products(activations, grad_out, ((2, 0), (2, 1)), grad_ready=False)
    lower, upper = to_neighbours(far)
    direct = products(activations, grad, ((1, 0), (3, 1)))
    direct_came = to_neighbours(direct)
    passed = products(activations, grad, after)
    upper, lower = to_neighbours(relayed(passed, (upper, lower)))
    kept = products(activations, grad, own, base=direct_came)
    mine, *sent = summed(*kept, lower, upper)
    for value, s in zip(sent, ORDER):
        mine = mine + sent_over(value, s, 1)
    mine = (mine * grad_scale).reshape(SIDE, 2, ROWS, COLS)
    kept = taken(mine, core, 1)
    came = exchanged(taken(mine, core ^ 1, 1), "group", 1)
    both = jnp.where(core == 0, jnp.stack([kept, came], 1), jnp.stack([came, kept], 1))
    blocks = [taken(both, y, 0)]
    for s in (1, 2, 3):
        blocks.append(exchanged(taken(both, y ^ s, 0), "group", 2 * s))
    sums, ordered = pl.pallas_call(
        gram_kernel,
        in_specs=[pl.BlockSpec(memory_space=pltpu.SMEM)] + in_vmem(SIDE),
        out_specs=in_vmem(2),
        out_shape=[
            jax.ShapeDtypeStruct((TOTAL, 128), jnp.float32),
            jax.ShapeDtypeStruct((GROUPS, ROWS, COLS), jnp.float32),
        ],
        compiler_params=pltpu.CompilerParams(vmem_limit_bytes=4 << 20),
        name="gram",
    )(y.reshape(1).astype(jnp.int32), *blocks)
    sums = lax.all_to_all(sums, ("blk", "group"), split_axis=0, concat_axis=0, tiled=True)
    return tuple(
        pl.pallas_call(
            finish_kernel,
            in_specs=in_vmem(4),
            out_specs=in_vmem(2),
            out_shape=[jax.ShapeDtypeStruct(weights.shape, jnp.float32)] * 2,
            compiler_params=pltpu.CompilerParams(vmem_limit_bytes=4 << 20),
            name="finish",
        )(sums, ordered, weights, momentum)
    )


def solution(mesh):
    spec = P(("blk", "group"), None)
    return jax.shard_map(
        shards, mesh=mesh, in_specs=(spec,) * 4, out_specs=(spec,) * 2, check_vma=False
    )
```

```python
import functools
import math

import jax
import jax.numpy as jnp
from jax import lax
from jax.experimental import pallas as pl
from jax.experimental.pallas import tpu as pltpu
from jax.sharding import PartitionSpec as P

EPSILON = 1e-06
GROUPS = 8
SIDE = 4
ROWS = 16
COLS = 512
PIECE = GROUPS * ROWS
DEPTH = 512
HEAD = 4
ORDER = (2, 1, 3)
TOTAL = 128
CONTRACT = (((0,), (0,)), ((), ()))


def exchanged(value, axis, mask):
    return lax.ppermute(value, axis, [(k, k ^ mask) for k in range(lax.axis_size(axis))])


def in_vmem(count):
    return [pl.BlockSpec(memory_space=pltpu.VMEM)] * count


def my_place():
    blk, core = lax.axis_index("blk"), lax.axis_index("group") % 2
    x, z = blk // SIDE, blk % SIDE
    return jnp.where(core == 0, x, z), jnp.where(core == 0, z, x), core


def piece_blocks(units):
    first, _, core = my_place()
    return [
        jnp.where(core == 0, (first ^ s) * SIDE + k, k * SIDE + (first ^ s))
        for s, h in units
        for k in (2 * h, 2 * h + 1)
    ]


def way_pairs(s, half):
    along_x = [core == half for core in range(2)]
    return [
        (k, k ^ (GROUPS * s * (SIDE if along_x[k % 2] else 1))) for k in range(TOTAL)
    ]


def sent_over(value, s, half):
    return lax.ppermute(value, ("blk", "group"), way_pairs(s, half))


def product_kernel(units, later, head_ready, grad_ready, based, *refs):
    refs = list(refs)
    act_ref, out_ref = refs.pop(0), refs.pop(0)
    head = refs.pop(0) if head_ready else None
    base = [refs.pop(0) for _ in units] if based else ()
    pieces = [refs.pop(0) for _ in units]
    grad = out_ref if grad_ready else refs.pop(0)
    later_head = refs.pop(0) if later else None
    held, sems = refs
    chunks = grad.shape[0] // DEPTH
    copies = []

    def start(units, held, k, with_grad):
        rows = pl.ds(k * DEPTH, DEPTH)
        ends = [(out_ref.at[rows], grad.at[rows])] if with_grad else []
        for c, block in enumerate(piece_blocks(units) if units else ()):
            columns = pl.ds(pl.multiple_of(block * PIECE, PIECE), PIECE)
            ends.append((act_ref.at[rows, columns], held.at[rows, pl.ds(c * PIECE, PIECE)]))
        copies.append(
            [
                pltpu.make_async_copy(source, target, sems.at[len(copies), place])
                for place, (source, target) in enumerate(ends)
            ]
        )
        for copy in copies[-1]:
            copy.start()

    for k in range(chunks):
        start(() if head_ready and k < HEAD else units, held, k, not grad_ready)
    if later:
        for k in range(HEAD):
            start(later, later_head, k, False)
    for k in range(chunks):
        for copy in copies[k]:
            copy.wait()
        rows = pl.ds(k * DEPTH, DEPTH)
        source = head if head_ready and k < HEAD else held
        part = lax.dot_general(source[rows], grad[rows], CONTRACT, preferred_element_type=jnp.float32)
        for n, piece in enumerate(pieces):
            mine = part[n * 2 * PIECE : (n + 1) * 2 * PIECE]
            if k:
                piece[...] += mine
            elif based:
                piece[...] = base[n][...] + mine
            else:
                piece[...] = mine
    for chunk in copies[chunks:]:
        for copy in chunk:
            copy.wait()


def products(activations, grad_out, units, later=(), head=None, grad_ready=True, base=()):
    tokens, cols = grad_out.shape
    width = 2 * PIECE * len(units)
    outs = [jax.ShapeDtypeStruct((2 * PIECE, cols), jnp.float32)] * len(units)
    outs += [] if grad_ready else [jax.ShapeDtypeStruct((tokens, cols), grad_out.dtype)]
    outs += [jax.ShapeDtypeStruct((HEAD * DEPTH, width), activations.dtype)] if later else []
    out_space = pltpu.VMEM if grad_ready else pltpu.HBM
    ready = [] if head is None else [pltpu.with_memory_space_constraint(head, pltpu.VMEM)]
    return pl.pallas_call(
        functools.partial(product_kernel, units, later, bool(ready), grad_ready, bool(base)),
        in_specs=[
            pl.BlockSpec(memory_space=pl.ANY),
            pl.BlockSpec(memory_space=pltpu.VMEM if grad_ready else pl.ANY),
        ]
        + in_vmem(len(ready) + len(base)),
        out_specs=in_vmem(len(outs)),
        out_shape=outs,
        scratch_shapes=[
            pltpu.VMEM((tokens, width), activations.dtype),
            pltpu.SemaphoreType.DMA((tokens // DEPTH + HEAD, 1 + 2 * len(units))),
        ],
        compiler_params=pltpu.CompilerParams(vmem_limit_bytes=24 << 20),
        cost_estimate=pl.CostEstimate(flops=1000, bytes_accessed=1000, transcendentals=0),
        name="products",
    )(
        pltpu.with_memory_space_constraint(activations, pltpu.HBM),
        pltpu.with_memory_space_constraint(grad_out, out_space),
        *ready,
        *base,
    )


def relayed_kernel(*refs):
    for one_ref, other_ref, out_ref in zip(refs[:2], refs[2:4], refs[4:]):
        out_ref[...] = one_ref[...] + other_ref[...]


def relayed(own, came):
    return pl.pallas_call(
        relayed_kernel,
        in_specs=in_vmem(4),
        out_specs=in_vmem(2),
        out_shape=[jax.ShapeDtypeStruct(value.shape, value.dtype) for value in own],
        compiler_params=pltpu.CompilerParams(vmem_limit_bytes=8 << 20),
        cost_estimate=pl.CostEstimate(flops=1000, bytes_accessed=1000, transcendentals=0),
        name="relayed",
    )(*own, *came)


def summed_kernel(own_lower_ref, own_upper_ref, lower_ref, upper_ref, *out_refs):
    _, second, _ = my_place()
    for out_ref, s in zip(out_refs, (0, *ORDER)):
        place = second ^ s
        rows = pl.ds(pl.multiple_of((place & 1) * PIECE, PIECE), PIECE)

        @pl.when(place < 2)
        def _():
            out_ref[...] = own_lower_ref[rows] + lower_ref[rows]

        @pl.when(place >= 2)
        def _():
            out_ref[...] = own_upper_ref[rows] + upper_ref[rows]


def summed(*values):
    return pl.pallas_call(
        summed_kernel,
        in_specs=in_vmem(4),
        out_specs=in_vmem(4),
        out_shape=[jax.ShapeDtypeStruct((PIECE, COLS), jnp.float32)] * 4,
        compiler_params=pltpu.CompilerParams(vmem_limit_bytes=8 << 20),
        name="summed",
    )(*values)


def pair_slots():
    return [(i, j) for i in range(GROUPS) for j in range(i, GROUPS)]


def gram_kernel(place_ref, *refs):
    *block_refs, sums_ref, ordered_ref = refs
    y = place_ref[0]
    slots = [[block_ref[core] for core in range(2)] for block_ref in block_refs]
    for bit in (1, 2):
        moved = (y & bit) != 0
        slots = [
            [jnp.where(moved, slots[k ^ bit][core], slots[k][core]) for core in range(2)]
            for k in range(SIDE)
        ]
    groups = [slots[i // 2][i % 2] for i in range(GROUPS)]
    for i in range(GROUPS):
        ordered_ref[i] = groups[i]
    rows = []
    for i, j in pair_slots():
        product = groups[i] * groups[j]
        product = product[:8] + product[8:]
        product = product[:, :256] + product[:, 256:]
        product = product[:, :128] + product[:, 128:]
        rows.append(jnp.sum(product, axis=0, keepdims=True))
    rows.append(jnp.zeros((128 - len(rows), 128), jnp.float32))
    sums_ref[...] = lax.dot_general(
        jnp.ones((TOTAL, 128), jnp.float32),
        jnp.concatenate(rows, axis=0),
        (((1,), (1,)), ((), ())),
        precision=lax.Precision.HIGHEST,
        preferred_element_type=jnp.float32,
    )


def finish_kernel(sums_ref, ordered_ref, weights_ref, momentum_ref, new_weights_ref, new_momentum_ref):
    sums = jnp.sum(sums_ref[...], axis=0, keepdims=True)
    gram = {}
    for place, (i, j) in enumerate(pair_slots()):
        gram[i, j] = gram[j, i] = sums[:, place : place + 1]
    shares = [1.0] * GROUPS
    count = GROUPS
    while count > 1:
        half = count // 2
        coef = [None] * count
        for i in range(half):
            cross = gram[i, i + half]
            coef[i] = 1.0 - cross / (2.0 * (jnp.maximum(gram[i, i], 0.0) + EPSILON))
            coef[i + half] = 1.0 - cross / (2.0 * (jnp.maximum(gram[i + half, i + half], 0.0) + EPSILON))
        shares = [shares[g] * coef[g % count] for g in range(GROUPS)]
        later = {}
        for i in range(half):
            for j in range(i, half):
                later[i, j] = later[j, i] = (
                    coef[i] * coef[j] * gram[i, j]
                    + coef[i + half] * coef[j + half] * gram[i + half, j + half]
                ) + (
                    coef[i] * coef[j + half] * gram[i, j + half]
                    + coef[i + half] * coef[j] * gram[i + half, j]
                )
        gram = later
        count = half
    combined = shares[0] * ordered_ref[0]
    for i in range(1, GROUPS):
        combined = combined + shares[i] * ordered_ref[i]
    new_momentum = 0.9 * momentum_ref[...] + combined
    new_momentum_ref[...] = new_momentum
    new_weights_ref[...] = (1.0 - 0.1 * 0.1) * weights_ref[...] - 0.1 * new_momentum


def shards(activations, grad_out, weights, momentum):
    group = lax.axis_index("group")
    y, core = group // 2, group % 2
    grad_scale = 1.0 / math.sqrt(activations.shape[0] * lax.axis_size("blk"))

    def taken(value, index, dim):
        return lax.dynamic_index_in_dim(value, index, dim, keepdims=False)

    def to_neighbours(pair):
        return sent_over(pair[0], 1, 0), sent_over(pair[1], 3, 0)

    near, after, own = ((1, 0), (3, 1)), ((1, 1), (3, 0)), ((0, 0), (0, 1))
    *far, grad, head = products(activations, grad_out, ((2, 0), (2, 1)), near, grad_ready=False)
    lower, upper = to_neighbours(far)
    *direct, head = products(activations, grad, near, after, head)
    direct_came = to_neighbours(direct)
    passed = products(activations, grad, after, head=head)
    upper, lower = to_neighbours(relayed(passed, (upper, lower)))
    kept = products(activations, grad, own, base=direct_came)
    mine, *sent = summed(*kept, lower, upper)
    for value, s in zip(sent, ORDER):
        mine = mine + sent_over(value, s, 1)
    mine = (mine * grad_scale).reshape(SIDE, 2, ROWS, COLS)
    kept = taken(mine, core, 1)
    came = exchanged(taken(mine, core ^ 1, 1), "group", 1)
    both = jnp.where(core == 0, jnp.stack([kept, came], 1), jnp.stack([came, kept], 1))
    blocks = [taken(both, y, 0)]
    for s in (1, 2, 3):
        blocks.append(exchanged(taken(both, y ^ s, 0), "group", 2 * s))
    sums, ordered = pl.pallas_call(
        gram_kernel,
        in_specs=[pl.BlockSpec(memory_space=pltpu.SMEM)] + in_vmem(SIDE),
        out_specs=in_vmem(2),
        out_shape=[
            jax.ShapeDtypeStruct((TOTAL, 128), jnp.float32),
            jax.ShapeDtypeStruct((GROUPS, ROWS, COLS), jnp.float32),
        ],
        compiler_params=pltpu.CompilerParams(vmem_limit_bytes=4 << 20),
        name="gram",
    )(y.reshape(1).astype(jnp.int32), *blocks)
    sums = lax.all_to_all(sums, ("blk", "group"), split_axis=0, concat_axis=0, tiled=True)
    return tuple(
        pl.pallas_call(
            finish_kernel,
            in_specs=in_vmem(4),
            out_specs=in_vmem(2),
            out_shape=[jax.ShapeDtypeStruct(weights.shape, jnp.float32)] * 2,
            compiler_params=pltpu.CompilerParams(vmem_limit_bytes=4 << 20),
            name="finish",
        )(sums, ordered, weights, momentum)
    )


def solution(mesh):
    spec = P(("blk", "group"), None)
    return jax.shard_map(
        shards, mesh=mesh, in_specs=(spec,) * 4, out_specs=(spec,) * 2, check_vma=False
    )
```

```python
import functools
import math

import jax
import jax.numpy as jnp
from jax import lax
from jax.experimental import pallas as pl
from jax.experimental.pallas import tpu as pltpu
from jax.sharding import PartitionSpec as P

EPSILON = 1e-06
GROUPS = 8
SIDE = 4
ROWS = 16
COLS = 512
PIECE = GROUPS * ROWS
DEPTH = 512
HEAD = 6
ORDER = (2, 1, 3)
TOTAL = 128
CONTRACT = (((0,), (0,)), ((), ()))


def exchanged(value, axis, mask):
    return lax.ppermute(value, axis, [(k, k ^ mask) for k in range(lax.axis_size(axis))])


def in_vmem(count):
    return [pl.BlockSpec(memory_space=pltpu.VMEM)] * count


def my_place():
    blk, core = lax.axis_index("blk"), lax.axis_index("group") % 2
    x, z = blk // SIDE, blk % SIDE
    return jnp.where(core == 0, x, z), jnp.where(core == 0, z, x), core


def piece_blocks(units):
    first, _, core = my_place()
    return [
        jnp.where(core == 0, (first ^ s) * SIDE + k, k * SIDE + (first ^ s))
        for s, h in units
        for k in (2 * h, 2 * h + 1)
    ]


def way_pairs(s, half):
    along_x = [core == half for core in range(2)]
    return [
        (k, k ^ (GROUPS * s * (SIDE if along_x[k % 2] else 1))) for k in range(TOTAL)
    ]


def sent_over(value, s, half):
    return lax.ppermute(value, ("blk", "group"), way_pairs(s, half))


def product_kernel(units, later, head_ready, grad_ready, based, *refs):
    refs = list(refs)
    act_ref, out_ref = refs.pop(0), refs.pop(0)
    head = refs.pop(0) if head_ready else None
    base = [refs.pop(0) for _ in units] if based else ()
    pieces = [refs.pop(0) for _ in units]
    grad = out_ref if grad_ready else refs.pop(0)
    later_head = refs.pop(0) if later else None
    held, sems = refs
    chunks = grad.shape[0] // DEPTH
    copies = []

    def start(units, held, k, with_grad):
        rows = pl.ds(k * DEPTH, DEPTH)
        ends = [(out_ref.at[rows], grad.at[rows])] if with_grad else []
        for c, block in enumerate(piece_blocks(units) if units else ()):
            columns = pl.ds(pl.multiple_of(block * PIECE, PIECE), PIECE)
            ends.append((act_ref.at[rows, columns], held.at[rows, pl.ds(c * PIECE, PIECE)]))
        copies.append(
            [
                pltpu.make_async_copy(source, target, sems.at[len(copies), place])
                for place, (source, target) in enumerate(ends)
            ]
        )
        for copy in copies[-1]:
            copy.start()

    for k in range(chunks):
        start(() if head_ready and k < HEAD else units, held, k, not grad_ready)
    if later:
        for k in range(HEAD):
            start(later, later_head, k, False)
    for k in range(chunks):
        for copy in copies[k]:
            copy.wait()
        rows = pl.ds(k * DEPTH, DEPTH)
        source = head if head_ready and k < HEAD else held
        part = lax.dot_general(source[rows], grad[rows], CONTRACT, preferred_element_type=jnp.float32)
        for n, piece in enumerate(pieces):
            mine = part[n * 2 * PIECE : (n + 1) * 2 * PIECE]
            if k:
                piece[...] += mine
            elif based:
                piece[...] = base[n][...] + mine
            else:
                piece[...] = mine
    for chunk in copies[chunks:]:
        for copy in chunk:
            copy.wait()


def products(activations, grad_out, units, later=(), head=None, grad_ready=True, base=()):
    tokens, cols = grad_out.shape
    width = 2 * PIECE * len(units)
    outs = [jax.ShapeDtypeStruct((2 * PIECE, cols), jnp.float32)] * len(units)
    outs += [] if grad_ready else [jax.ShapeDtypeStruct((tokens, cols), grad_out.dtype)]
    outs += [jax.ShapeDtypeStruct((HEAD * DEPTH, width), activations.dtype)] if later else []
    out_space = pltpu.VMEM if grad_ready else pltpu.HBM
    ready = [] if head is None else [pltpu.with_memory_space_constraint(head, pltpu.VMEM)]
    return pl.pallas_call(
        functools.partial(product_kernel, units, later, bool(ready), grad_ready, bool(base)),
        in_specs=[
            pl.BlockSpec(memory_space=pl.ANY),
            pl.BlockSpec(memory_space=pltpu.VMEM if grad_ready else pl.ANY),
        ]
        + in_vmem(len(ready) + len(base)),
        out_specs=in_vmem(len(outs)),
        out_shape=outs,
        scratch_shapes=[
            pltpu.VMEM((tokens, width), activations.dtype),
            pltpu.SemaphoreType.DMA((tokens // DEPTH + HEAD, 1 + 2 * len(units))),
        ],
        compiler_params=pltpu.CompilerParams(vmem_limit_bytes=24 << 20),
        cost_estimate=pl.CostEstimate(flops=1000, bytes_accessed=1000, transcendentals=0),
        name="products",
    )(
        pltpu.with_memory_space_constraint(activations, pltpu.HBM),
        pltpu.with_memory_space_constraint(grad_out, out_space),
        *ready,
        *base,
    )


def relayed_kernel(*refs):
    for one_ref, other_ref, out_ref in zip(refs[:2], refs[2:4], refs[4:]):
        out_ref[...] = one_ref[...] + other_ref[...]


def relayed(own, came):
    return pl.pallas_call(
        relayed_kernel,
        in_specs=in_vmem(4),
        out_specs=in_vmem(2),
        out_shape=[jax.ShapeDtypeStruct(value.shape, value.dtype) for value in own],
        compiler_params=pltpu.CompilerParams(vmem_limit_bytes=8 << 20),
        cost_estimate=pl.CostEstimate(flops=1000, bytes_accessed=1000, transcendentals=0),
        name="relayed",
    )(*own, *came)


def summed_kernel(own_lower_ref, own_upper_ref, lower_ref, upper_ref, *out_refs):
    _, second, _ = my_place()
    for out_ref, s in zip(out_refs, (0, *ORDER)):
        place = second ^ s
        rows = pl.ds(pl.multiple_of((place & 1) * PIECE, PIECE), PIECE)

        @pl.when(place < 2)
        def _():
            out_ref[...] = own_lower_ref[rows] + lower_ref[rows]

        @pl.when(place >= 2)
        def _():
            out_ref[...] = own_upper_ref[rows] + upper_ref[rows]


def summed(*values):
    return pl.pallas_call(
        summed_kernel,
        in_specs=in_vmem(4),
        out_specs=in_vmem(4),
        out_shape=[jax.ShapeDtypeStruct((PIECE, COLS), jnp.float32)] * 4,
        compiler_params=pltpu.CompilerParams(vmem_limit_bytes=8 << 20),
        name="summed",
    )(*values)


def pair_slots():
    return [(i, j) for i in range(GROUPS) for j in range(i, GROUPS)]


def gram_kernel(place_ref, *refs):
    *block_refs, sums_ref, ordered_ref = refs
    y = place_ref[0]
    slots = [[block_ref[core] for core in range(2)] for block_ref in block_refs]
    for bit in (1, 2):
        moved = (y & bit) != 0
        slots = [
            [jnp.where(moved, slots[k ^ bit][core], slots[k][core]) for core in range(2)]
            for k in range(SIDE)
        ]
    groups = [slots[i // 2][i % 2] for i in range(GROUPS)]
    for i in range(GROUPS):
        ordered_ref[i] = groups[i]
    rows = []
    for i, j in pair_slots():
        product = groups[i] * groups[j]
        product = product[:8] + product[8:]
        product = product[:, :256] + product[:, 256:]
        product = product[:, :128] + product[:, 128:]
        rows.append(jnp.sum(product, axis=0, keepdims=True))
    rows.append(jnp.zeros((128 - len(rows), 128), jnp.float32))
    sums_ref[...] = lax.dot_general(
        jnp.ones((TOTAL, 128), jnp.float32),
        jnp.concatenate(rows, axis=0),
        (((1,), (1,)), ((), ())),
        precision=lax.Precision.HIGHEST,
        preferred_element_type=jnp.float32,
    )


def finish_kernel(sums_ref, ordered_ref, weights_ref, momentum_ref, new_weights_ref, new_momentum_ref):
    sums = jnp.sum(sums_ref[...], axis=0, keepdims=True)
    gram = {}
    for place, (i, j) in enumerate(pair_slots()):
        gram[i, j] = gram[j, i] = sums[:, place : place + 1]
    shares = [1.0] * GROUPS
    count = GROUPS
    while count > 1:
        half = count // 2
        coef = [None] * count
        for i in range(half):
            cross = gram[i, i + half]
            coef[i] = 1.0 - cross / (2.0 * (jnp.maximum(gram[i, i], 0.0) + EPSILON))
            coef[i + half] = 1.0 - cross / (2.0 * (jnp.maximum(gram[i + half, i + half], 0.0) + EPSILON))
        shares = [shares[g] * coef[g % count] for g in range(GROUPS)]
        later = {}
        for i in range(half):
            for j in range(i, half):
                later[i, j] = later[j, i] = (
                    coef[i] * coef[j] * gram[i, j]
                    + coef[i + half] * coef[j + half] * gram[i + half, j + half]
                ) + (
                    coef[i] * coef[j + half] * gram[i, j + half]
                    + coef[i + half] * coef[j] * gram[i + half, j]
                )
        gram = later
        count = half
    combined = shares[0] * ordered_ref[0]
    for i in range(1, GROUPS):
        combined = combined + shares[i] * ordered_ref[i]
    new_momentum = 0.9 * momentum_ref[...] + combined
    new_momentum_ref[...] = new_momentum
    new_weights_ref[...] = (1.0 - 0.1 * 0.1) * weights_ref[...] - 0.1 * new_momentum


def shards(activations, grad_out, weights, momentum):
    group = lax.axis_index("group")
    y, core = group // 2, group % 2
    grad_scale = 1.0 / math.sqrt(activations.shape[0] * lax.axis_size("blk"))

    def taken(value, index, dim):
        return lax.dynamic_index_in_dim(value, index, dim, keepdims=False)

    def to_neighbours(pair):
        return sent_over(pair[0], 1, 0), sent_over(pair[1], 3, 0)

    near, after, own = ((1, 0), (3, 1)), ((1, 1), (3, 0)), ((0, 0), (0, 1))
    *far, grad, head = products(activations, grad_out, ((2, 0), (2, 1)), near, grad_ready=False)
    lower, upper = to_neighbours(far)
    *direct, head = products(activations, grad, near, after, head)
    direct_came = to_neighbours(direct)
    passed = products(activations, grad, after, head=head)
    upper, lower = to_neighbours(relayed(passed, (upper, lower)))
    kept = products(activations, grad, own, base=direct_came)
    mine, *sent = summed(*kept, lower, upper)
    for value, s in zip(sent, ORDER):
        mine = mine + sent_over(value, s, 1)
    mine = (mine * grad_scale).reshape(SIDE, 2, ROWS, COLS)
    kept = taken(mine, core, 1)
    came = exchanged(taken(mine, core ^ 1, 1), "group", 1)
    both = jnp.where(core == 0, jnp.stack([kept, came], 1), jnp.stack([came, kept], 1))
    blocks = [taken(both, y, 0)]
    for s in (1, 2, 3):
        blocks.append(exchanged(taken(both, y ^ s, 0), "group", 2 * s))
    sums, ordered = pl.pallas_call(
        gram_kernel,
        in_specs=[pl.BlockSpec(memory_space=pltpu.SMEM)] + in_vmem(SIDE),
        out_specs=in_vmem(2),
        out_shape=[
            jax.ShapeDtypeStruct((TOTAL, 128), jnp.float32),
            jax.ShapeDtypeStruct((GROUPS, ROWS, COLS), jnp.float32),
        ],
        compiler_params=pltpu.CompilerParams(vmem_limit_bytes=4 << 20),
        name="gram",
    )(y.reshape(1).astype(jnp.int32), *blocks)
    sums = lax.all_to_all(sums, ("blk", "group"), split_axis=0, concat_axis=0, tiled=True)
    return tuple(
        pl.pallas_call(
            finish_kernel,
            in_specs=in_vmem(4),
            out_specs=in_vmem(2),
            out_shape=[jax.ShapeDtypeStruct(weights.shape, jnp.float32)] * 2,
            compiler_params=pltpu.CompilerParams(vmem_limit_bytes=4 << 20),
            name="finish",
        )(sums, ordered, weights, momentum)
    )


def solution(mesh):
    spec = P(("blk", "group"), None)
    return jax.shard_map(
        shards, mesh=mesh, in_specs=(spec,) * 4, out_specs=(spec,) * 2, check_vma=False
    )
```
